32 devices in a mesh: lat: 4 (over x, core), lon: 8 (over z, y).
Axes of the slice: x: 2, y: 2, z: 4, core: 2. Of those that a mesh axis runs over, the one named last changes fastest.
Arguments:
- control: float32 [20, 4, 64, 1024], P(None, None, 'lat', 'lon'), may hold values from -6 to 6
- kappa: float32 [64, 1024], P('lat', 'lon'), may hold values from 0.05 to 0.49
- sea_mask: int32 [64, 1024], P('lat', 'lon'), may hold values 0 or 1
- vert_coef: float32 [20, 64, 1024], P(None, 'lat', 'lon'), may hold values from 0.5 to 20
- stencil_offsets: int32 [8, 1024, 1024], P(None, ('lat', 'lon')), may hold values from 0 to 2047
- stencil_weights: float32 [8, 1024, 1024], P(None, ('lat', 'lon')), may hold values from 0.05 to 0.3
- slot_target: int32 [1024, 1024], P(('lat', 'lon')), may hold values from 0 to 8191
- observed: float32 [262144], P(('lat', 'lon')), may hold values from -6 to 6
- inv_error: float32 [262144], P(('lat', 'lon')), may hold values from 0.5 to 2
Outputs:
- increment: float32 [20, 4, 64, 1024], P(None, None, 'lat', 'lon')
- misfit: float32 [262144], P(('lat', 'lon'))
The draws below stay inside these ranges and needn't reach their ends.
Inputs may be any that keep to these rules, and one draw needn't show every extreme that they name: `stencil_offsets`: an offset indexes one horizontal cell of one device's tile, as row * 128 + column.
All inputs are finite; a program needn't handle non-finite values. No bound on the sum of `sea_mask` on one device may be relied on, other than what follows from the above.
Results may differ from the reference program's by a relative error of at most 0.00002.
Values sent between devices are 32-bit elements; how exact they have to be, the bound alone decides.
A program may use at most 64 MiB of HBM per device.

```python
import math
import jax
import jax.numpy as jnp
from jax import lax

FIELDS = 4
LEV = 20
CLAT = 16
CLON = 128
STEPS = 10
STEN = 8
CAP = 1024
OWN = 8192
NLAT = 64
NLON = 1024
PAIRS = 1024
OBS = 262144
N_LAT = 4
N_LON = 8


def place_ends(values, stream_key, smallest, high):
    longest = values.shape.index(max(values.shape))
    spots = []
    for shift in (0, 1):
        where = [jax.random.randint(jax.random.fold_in(stream_key, axis), (), 0, length) for axis, length in enumerate(values.shape)]
        where[longest] = (where[longest] + shift) % values.shape[longest]
        spots.append(tuple(where))
    return values.at[spots[0]].set(smallest).at[spots[1]].set(high)


def block_levels(rng, dims, split, low, top_value):
    level, own = 1.0, jax.random.fold_in(rng, 6)
    for dim, parts in split:
        heights = jnp.exp(jax.random.uniform(jax.random.fold_in(own, dim), (parts,), jnp.float32, low / len(split), top_value / len(split)))
        level = level * jnp.repeat(heights, dims[dim] // parts).reshape([-1 if axis == dim else 1 for axis in range(len(dims))])
    return level


def noise(rng, shape, width, bound, split=(), kind=jnp.bfloat16):
    values = jax.random.normal(rng, shape, jnp.float32) * width
    if len(split) > 0:
        values = block_levels(rng, shape, split, -0.22, 0.18) * values
    return jnp.clip(values, min=-bound, max=bound).astype(kind)


def setup_inputs(seed: int = 0) -> dict:
    key_list = jax.random.split(jax.random.key(seed), 10)
    control = noise(key_list[0], (LEV, FIELDS, NLAT, NLON), 1.0, 6.0, ((2, 4), (3, 8)), jnp.float32)
    kappa = jnp.clip(jnp.exp(math.log(0.49) - 2.2823824 * jax.random.uniform(key_list[1], (NLAT, NLON), jnp.float32) ** block_levels(key_list[1], (NLAT, NLON), ((0, 4), (1, 8)), -0.2, 0.2)), 0.05, 0.49)
    sea_mask = place_ends((jax.random.randint(key_list[2], (NLAT, NLON), 0, 5) < 4).astype(jnp.int32), jax.random.fold_in(key_list[2], 1), 0, 1)
    vert_coef = jnp.clip(jnp.exp(math.log(20.0) - 3.6888795 * jax.random.uniform(key_list[3], (LEV, NLAT, NLON), jnp.float32) ** block_levels(key_list[3], (LEV, NLAT, NLON), ((1, 4), (2, 8)), -0.2, 0.2)), 0.5, 20.0)
    stencil_offsets = place_ends(jax.random.randint(key_list[4], (STEN, PAIRS, CAP), 0, CLAT * CLON), jax.random.fold_in(key_list[4], 1), 0, (CLAT * CLON) - 1).astype(jnp.int32)
    stencil_weights = jnp.clip(0.05 + 0.25 * jax.random.uniform(key_list[5], (STEN, PAIRS, CAP), jnp.float32) ** block_levels(key_list[5], (STEN, PAIRS, CAP), ((1, 32),), -0.2, 0.2), 0.05, 0.3)
    slot_target = place_ends(jax.random.randint(key_list[6], (PAIRS, CAP), 0, OWN), jax.random.fold_in(key_list[6], 1), 0, OWN - 1).astype(jnp.int32)
    observed = noise(key_list[7], (OBS,), 1.0, 6.0, ((0, 32),), jnp.float32)
    inv_error = jnp.clip(jnp.exp(math.log(2.0) - 1.3862944 * jax.random.uniform(key_list[8], (OBS,), jnp.float32) ** block_levels(key_list[8], (OBS,), ((0, 32),), -0.2, 0.2)), 0.5, 2.0)
    return dict(control=control, kappa=kappa, sea_mask=sea_mask, vert_coef=vert_coef, stencil_offsets=stencil_offsets, stencil_weights=stencil_weights, slot_target=slot_target, observed=observed, inv_error=inv_error)


def diffuse_step(wide, gwide):
    centre = wide[:, 1:-1, 1:-1]
    flux = gwide[2:, 1:-1] * (wide[:, 2:, 1:-1] - centre)
    flux = flux + gwide[:-2, 1:-1] * (wide[:, :-2, 1:-1] - centre)
    flux = flux + gwide[1:-1, 2:] * (wide[:, 1:-1, 2:] - centre)
    flux = flux + gwide[1:-1, :-2] * (wide[:, 1:-1, :-2] - centre)
    return centre + gwide[1:-1, 1:-1] * flux


def column_solve(rhs, vert_coef):
    upper_coef = jnp.concatenate([vert_coef[1:], jnp.zeros_like(vert_coef[:1])], axis=0)
    diag = 1.0 + vert_coef + upper_coef
    lower = -vert_coef
    upper = -upper_coef

    def forward(carry, items):
        cprev, dprev = carry
        low, mid, up, right = items
        denom = mid - low * cprev
        cnew = up / denom
        dnew = (right - low[None] * dprev) / denom[None]
        return (cnew, dnew), (cnew, dnew)

    init = (jnp.zeros(rhs.shape[2:], jnp.float32), jnp.zeros(rhs.shape[1:], jnp.float32))
    _, (cstore, dstore) = lax.scan(forward, init, (lower, diag, upper, rhs))

    def backward(ynext, items):
        cval, dval = items
        yval = dval - cval[None] * ynext
        return yval, yval

    _, result = lax.scan(backward, jnp.zeros(rhs.shape[1:], jnp.float32), (cstore, dstore), reverse=True)
    return result


def reference(control, kappa, sea_mask, vert_coef, stencil_offsets, stencil_weights, slot_target, observed, inv_error):
    devices = N_LAT * N_LON
    coef = kappa * sea_mask.astype(jnp.float32)
    gwide = jnp.pad(coef, ((0, 0), (1, 1)), mode="wrap")
    gwide = jnp.pad(gwide, ((1, 1), (0, 0)))
    field = control.reshape(LEV * FIELDS, NLAT, NLON)
    for step in range(STEPS):
        wide = jnp.pad(field, ((0, 0), (0, 0), (1, 1)), mode="wrap")
        wide = jnp.pad(wide, ((0, 0), (1, 1), (0, 0)))
        field = diffuse_step(wide, gwide)
    increment = column_solve(field.reshape(LEV, FIELDS, NLAT, NLON), vert_coef)
    tiles = increment.reshape(LEV, FIELDS, N_LAT, CLAT, N_LON, CLON)
    tiles = tiles.transpose(2, 4, 0, 1, 3, 5).reshape(devices, LEV * FIELDS * CLAT * CLON)
    slot_index = jnp.arange(devices * CAP, dtype=jnp.int32) % CAP
    layer = (slot_index % (LEV * FIELDS)).astype(jnp.int32)
    offsets = stencil_offsets.reshape(STEN, devices, devices * CAP).astype(jnp.int32)
    offsets = offsets + (layer * (CLAT * CLON)).astype(jnp.int32)[None, None, :]
    weights = stencil_weights.reshape(STEN, devices, devices * CAP)
    values = jax.vmap(lambda tile, idx: tile[idx], in_axes=(0, 1), out_axes=1)(tiles, offsets)
    partial_value = jnp.sum(values * weights, axis=0).reshape(devices, devices, CAP)
    received = partial_value.transpose(1, 0, 2)
    owner = jnp.arange(devices, dtype=jnp.int32).reshape(devices, 1, 1)
    target = owner * OWN + slot_target.reshape(devices, devices, CAP)
    value = jnp.zeros((devices * OWN,), jnp.float32).at[target.reshape(-1)].add(received.reshape(-1))
    misfit = (value - observed) * inv_error
    return increment, misfit
```

```python
import functools

import jax
import jax.numpy as jnp
from jax import lax
from jax.experimental import pallas as pl
from jax.experimental.pallas import tpu as pltpu
from jax.sharding import PartitionSpec as P

STEPS = 10
LANES = 128
SUB = 8


def with_halo(cells, sides, width, closed):
    for axis, dim in sides:
        count = lax.axis_size(axis)
        ends = count if closed else count - 1
        head = lax.slice_in_dim(cells, 0, width, axis=dim)
        tail = lax.slice_in_dim(cells, cells.shape[dim] - width, cells.shape[dim], axis=dim)
        cells = jnp.concatenate(
            [
                lax.ppermute(tail, axis, [(i, (i + 1) % count) for i in range(ends)]),
                cells,
                lax.ppermute(head, axis, [((i + 1) % count, i) for i in range(ends)]),
            ],
            axis=dim,
        )
    return cells


def diffuse_step(wide, gwide):
    centre = wide[:, 1:-1, 1:-1]
    flux = gwide[2:, 1:-1] * (wide[:, 2:, 1:-1] - centre)
    flux = flux + gwide[:-2, 1:-1] * (wide[:, :-2, 1:-1] - centre)
    flux = flux + gwide[1:-1, 2:] * (wide[:, 1:-1, 2:] - centre)
    flux = flux + gwide[1:-1, :-2] * (wide[:, 1:-1, :-2] - centre)
    return centre + gwide[1:-1, 1:-1] * flux


def column_solve(rhs, vert_coef):
    upper_coef = jnp.concatenate([vert_coef[1:], jnp.zeros_like(vert_coef[:1])], axis=0)
    diag = 1.0 + vert_coef + upper_coef
    lower = -vert_coef
    upper = -upper_coef

    def forward(carry, items):
        cprev, dprev = carry
        low, mid, up, right = items
        denom = mid - low * cprev
        cnew = up / denom
        dnew = (right - low[None] * dprev) / denom[None]
        return ((cnew, dnew), (cnew, dnew))

    init = (jnp.zeros(rhs.shape[2:], jnp.float32), jnp.zeros(rhs.shape[1:], jnp.float32))
    _, (cstore, dstore) = lax.scan(forward, init, (lower, diag, upper, rhs))

    def backward(ynext, items):
        cval, dval = items
        yval = dval - cval[None] * ynext
        return (yval, yval)

    _, result = lax.scan(
        backward, jnp.zeros(rhs.shape[1:], jnp.float32), (cstore, dstore), reverse=True
    )
    return result


def pick(table, row, col):
    level = [jnp.take_along_axis(t, col, axis=1) for t in table]
    bit = 1
    while len(level) > 1:
        odd = (row & bit) != 0
        level = [jnp.where(odd, level[i + 1], level[i]) for i in range(0, len(level), 2)]
        bit *= 2
    return level[0]


def gather_kernel(rows, layers, owners, inc_ref, off_ref, w_ref, out_ref, off_t, w_t, acc):
    cap = off_ref.shape[1]
    groups = off_ref.shape[0] // LANES
    turns = -(-cap // layers)
    padded = turns * layers
    if padded > cap:
        for g in range(groups):
            off_t[g, cap:padded, :] = jnp.zeros((padded - cap, LANES), jnp.int32)
            w_t[g, cap:padded, :] = jnp.zeros((padded - cap, LANES), jnp.float32)
    for g in range(groups):
        for c in range(cap // LANES):
            here = pl.ds(c * LANES, LANES)
            off_t[g, here, :] = off_ref[pl.ds(g * LANES, LANES), here].T
            w_t[g, here, :] = w_ref[pl.ds(g * LANES, LANES), here].T

    def one_group(lg, carry):
        base = pl.multiple_of(lg * SUB, SUB)
        table = [inc_ref[pl.ds(base * rows + r, SUB, stride=rows), :] for r in range(rows)]
        for m in range(turns):
            at = pl.ds(m * layers + base, SUB)
            total = None
            for g in range(groups):
                idx = off_t[g, at, :]
                term = pick(table, idx >> 7, idx & (LANES - 1)) * w_t[g, at, :]
                total = term if total is None else total + term
            acc[at, :] = total
        return carry

    lax.fori_loop(0, layers // SUB, one_group, 0)
    for c in range(cap // LANES):
        here = pl.ds(c * LANES, LANES)
        block = acc[here, :].T
        total = block[:owners]
        for k in range(1, LANES // owners):
            total = total + block[k * owners : (k + 1) * owners]
        out_ref[:, here] = total


def gather_partials(increment, offsets, weights):
    layers, rows, cols = increment.shape
    sten, owners, cap = offsets.shape
    groups = sten * owners // LANES
    padded = -(-cap // layers) * layers
    return pl.pallas_call(
        functools.partial(gather_kernel, rows, layers, owners),
        out_shape=jax.ShapeDtypeStruct((owners, cap), jnp.float32),
        in_specs=[pl.BlockSpec(memory_space=pltpu.VMEM)] * 3,
        out_specs=pl.BlockSpec(memory_space=pltpu.VMEM),
        scratch_shapes=[
            pltpu.VMEM((groups, padded, LANES), jnp.int32),
            pltpu.VMEM((groups, padded, LANES), jnp.float32),
            pltpu.VMEM((padded, LANES), jnp.float32),
        ],
        compiler_params=pltpu.CompilerParams(vmem_limit_bytes=32 * 1024 * 1024),
        name="gather_partials",
    )(
        increment.reshape(layers * rows, cols),
        offsets.reshape(sten * owners, cap),
        weights.reshape(sten * owners, cap),
    )


def split_parts(v):
    first = v.astype(jnp.bfloat16).astype(jnp.float32)
    rest = v - first
    second = rest.astype(jnp.bfloat16).astype(jnp.float32)
    return first, second, rest - second


def spread(v, t, high):
    cap = v.shape[1]
    hit = lax.broadcasted_iota(jnp.int32, (high, cap), 0) == (t >> 7)
    ones = lax.broadcasted_iota(jnp.int32, (LANES, cap), 0) == (t & (LANES - 1))
    left = jnp.concatenate(
        [jnp.where(hit, part, 0.0).astype(jnp.bfloat16) for part in split_parts(v)], axis=0
    )
    right = jnp.where(ones, 1.0, 0.0).astype(jnp.bfloat16)
    return lax.dot_general(
        left, right, (((1,), (1,)), ((), ())), preferred_element_type=jnp.float32
    )


def scatter_kernel(rec_ref, tgt_ref, obs_ref, err_ref, out_ref, acc):
    high = obs_ref.shape[0]
    acc[...] = jnp.zeros_like(acc)

    def one_source(p, carry):
        acc[...] += spread(rec_ref[pl.ds(p, 1), :], tgt_ref[pl.ds(p, 1), :], high)
        return carry

    lax.fori_loop(0, rec_ref.shape[0], one_source, 0)
    total = acc[:high] + acc[high : 2 * high] + acc[2 * high :]
    out_ref[...] = (total - obs_ref[...]) * err_ref[...]


def scatter_misfit(received, target, observed, inv_error):
    high = observed.shape[0] // LANES
    out = pl.pallas_call(
        scatter_kernel,
        out_shape=jax.ShapeDtypeStruct((high, LANES), jnp.float32),
        in_specs=[pl.BlockSpec(memory_space=pltpu.VMEM)] * 4,
        out_specs=pl.BlockSpec(memory_space=pltpu.VMEM),
        scratch_shapes=[pltpu.VMEM((3 * high, LANES), jnp.float32)],
        compiler_params=pltpu.CompilerParams(vmem_limit_bytes=32 * 1024 * 1024),
        name="scatter_misfit",
    )(received, target, observed.reshape(high, LANES), inv_error.reshape(high, LANES))
    return out.reshape(-1)


def per_device(
    control,
    kappa,
    sea_mask,
    vert_coef,
    stencil_offsets,
    stencil_weights,
    slot_target,
    observed,
    inv_error,
):
    levels, fields, rows, cols = control.shape
    coef = kappa * sea_mask.astype(jnp.float32)
    field = control.reshape(levels * fields, rows, cols)
    depth = 1

    def one_round(turn, state):
        stacked = jnp.concatenate([state, coef[None]], axis=0)
        wide = with_halo(stacked, (("lon", 2),), depth, True)
        wide = with_halo(wide, (("lat", 1),), depth, False)
        inner = wide[:-1]
        gwide = wide[-1]
        inner = diffuse_step(inner, gwide)
        return inner

    field = lax.fori_loop(0, STEPS // depth, one_round, field)
    increment = column_solve(field.reshape(levels, fields, rows, cols), vert_coef)
    partial_value = gather_partials(
        increment.reshape(levels * fields, rows, cols), stencil_offsets, stencil_weights
    )
    received = lax.all_to_all(
        partial_value, ("lat", "lon"), split_axis=0, concat_axis=0, tiled=True
    )
    misfit = scatter_misfit(received, slot_target, observed, inv_error)
    return (increment, misfit)


def solution(mesh):
    return jax.shard_map(
        per_device,
        mesh=mesh,
        in_specs=(
            P(None, None, "lat", "lon"),
            P("lat", "lon"),
            P("lat", "lon"),
            P(None, "lat", "lon"),
            P(None, ("lat", "lon"), None),
            P(None, ("lat", "lon"), None),
            P(("lat", "lon"), None),
            P(("lat", "lon")),
            P(("lat", "lon")),
        ),
        out_specs=(P(None, None, "lat", "lon"), P(("lat", "lon"))),
        check_vma=False,
    )
```

```python
import functools

import jax
import jax.numpy as jnp
from jax import lax
from jax.experimental import pallas as pl
from jax.experimental.pallas import tpu as pltpu
from jax.sharding import PartitionSpec as P

STEPS = 10
LANES = 128
SUB = 8


def lane_ids():
    return lax.broadcasted_iota(jnp.int32, (SUB, LANES), 1)


def lay_kernel(rows, layers, field_ref, kappa_ref, mask_ref, out_ref):
    wide = layers + SUB
    coef = kappa_ref[...] * mask_ref[...].astype(jnp.float32)
    for r in range(rows):
        for g in range(layers // SUB):
            out_ref[pl.ds(r * wide + g * SUB, SUB), :] = field_ref[
                pl.ds(g * SUB * rows + r, SUB, stride=rows), :
            ]
        out_ref[pl.ds(r * wide + layers, SUB), :] = jnp.broadcast_to(
            coef[r : r + 1, :], (SUB, LANES)
        )


def pack_kernel(rows, groups, main_ref, north_ref, south_ref, head_ref, tail_ref):
    lane = lane_ids()
    pitch = LANES // groups
    wide = groups * SUB

    def pack(src, count, start):
        def one_row(r, carry):
            base = pl.multiple_of(r * wide, SUB)
            head = jnp.zeros((SUB, LANES), jnp.float32)
            tail = head
            for g in range(groups):
                cells = src[pl.ds(base + g * SUB, SUB), :]
                spot = (lane >= g * pitch) & (lane < g * pitch + STEPS)
                head = jnp.where(spot, pltpu.roll(cells, g * pitch, 1), head)
                move = (g * pitch + STEPS) % LANES
                tail = jnp.where(spot, pltpu.roll(cells, move, 1), tail)
            at = pl.ds(pl.multiple_of((start + r) * SUB, SUB), SUB)
            head_ref[at, :] = head
            tail_ref[at, :] = tail
            return carry

        lax.fori_loop(0, count, one_row, 0)

    pack(north_ref, STEPS, 0)
    pack(main_ref, rows, STEPS)
    pack(south_ref, STEPS, STEPS + rows)


def diffuse(rows, layers, main_ref, north_ref, south_ref, west_ref, east_ref, near, far, coefs):
    lane = lane_ids()
    groups = layers // SUB + 1
    pitch = LANES // groups
    wide = groups * SUB
    tall = rows + 2 * STEPS

    def outer(r, g):
        at = pl.ds(pl.multiple_of(r * SUB, SUB), SUB)
        east = pltpu.roll(east_ref[at, :], (LANES - g * pitch) % LANES, 1)
        west = pltpu.roll(west_ref[at, :], (2 * LANES - STEPS - g * pitch) % LANES, 1)
        return jnp.where(lane < STEPS, east, jnp.where(lane >= LANES - STEPS, west, 0.0))

    def fill(src, count, start):
        def one_row(r, carry):
            base = pl.multiple_of(r * wide, SUB)
            row = start + r
            for g in range(groups - 1):
                at = pl.ds(pl.multiple_of(row * layers + g * SUB, SUB), SUB)
                near[0, at, :] = src[pl.ds(base + g * SUB, SUB), :]
                far[0, at, :] = outer(row, g)
            at = pl.ds(pl.multiple_of(row * SUB, SUB), SUB)
            coefs[10, at, :] = src[pl.ds(base + layers, SUB), :]
            coefs[11, at, :] = outer(row, groups - 1)
            return carry

        lax.fori_loop(0, count, one_row, 0)

    fill(north_ref, STEPS, 0)
    fill(main_ref, rows, STEPS)
    fill(south_ref, STEPS, STEPS + rows)

    def sides(a, b):
        ra, rb = pltpu.roll(a, 1, 1), pltpu.roll(b, 1, 1)
        la, lb = pltpu.roll(a, LANES - 1, 1), pltpu.roll(b, LANES - 1, 1)
        first, last = lane == 0, lane == LANES - 1
        return (
            (jnp.where(first, rb, ra), jnp.where(last, lb, la)),
            (jnp.where(first, ra, rb), jnp.where(last, la, lb)),
        )

    def weigh(r, carry):
        at = pl.ds(pl.multiple_of(r * SUB, SUB), SUB)
        up = pl.ds(pl.multiple_of((r - 1) * SUB, SUB), SUB)
        down = pl.ds(pl.multiple_of((r + 1) * SUB, SUB), SUB)
        both = sides(coefs[10, at, :], coefs[11, at, :])
        for k in range(2):
            here = coefs[10 + k, at, :]
            n = here * coefs[10 + k, up, :]
            s = here * coefs[10 + k, down, :]
            w = here * both[k][0]
            e = here * both[k][1]
            coefs[5 * k, at, :] = 1.0 - ((n + s) + (w + e))
            coefs[5 * k + 1, at, :] = n
            coefs[5 * k + 2, at, :] = s
            coefs[5 * k + 3, at, :] = w
            coefs[5 * k + 4, at, :] = e
        return carry

    lax.fori_loop(1, tall - 1, weigh, 0)

    for step in range(STEPS):
        now, later = step % 2, (step + 1) % 2

        def one_row(r, carry, now=now, later=later):
            at = pl.ds(pl.multiple_of(r * SUB, SUB), SUB)
            c = [coefs[k, at, :] for k in range(10)]
            for g in range(groups - 1):
                mid = pl.ds(pl.multiple_of(r * layers + g * SUB, SUB), SUB)
                up = pl.ds(pl.multiple_of((r - 1) * layers + g * SUB, SUB), SUB)
                down = pl.ds(pl.multiple_of((r + 1) * layers + g * SUB, SUB), SUB)
                a, b = near[now, mid, :], far[now, mid, :]
                both = sides(a, b)
                for k, (buf, cells) in enumerate(((near, a), (far, b))):
                    p = c[5 * k : 5 * k + 5]
                    total = p[0] * cells + p[1] * buf[now, up, :]
                    other = p[3] * both[k][0] + p[4] * both[k][1]
                    buf[later, mid, :] = (total + p[2] * buf[now, down, :]) + other
            return carry

        lax.fori_loop(step + 1, tall - 1 - step, one_row, 0)


def solve_columns(rows, layers, near, vert_ref, inc_ref):
    levels = vert_ref.shape[0] // rows
    fields = layers // levels
    done = STEPS % 2
    for h in range(rows // SUB):
        ratio = []
        coef = vert_ref[pl.ds(h * SUB, SUB), :]
        cprev = jnp.zeros((SUB, LANES), jnp.float32)
        prev = [cprev] * fields
        for k in range(levels):
            if k + 1 < levels:
                below = vert_ref[pl.ds((k + 1) * rows + h * SUB, SUB), :]
            else:
                below = jnp.zeros((SUB, LANES), jnp.float32)
            inv = 1.0 / (((1.0 + coef) + below) + coef * cprev)
            cprev = -below * inv
            ratio.append(cprev)
            for f in range(fields):
                layer = k * fields + f
                right = near[done, pl.ds((STEPS + h * SUB) * layers + layer, SUB, stride=layers), :]
                prev[f] = (right + coef * prev[f]) * inv
                inc_ref[pl.ds(layer * rows + h * SUB, SUB), :] = prev[f]
            coef = below
        for k in range(levels - 2, -1, -1):
            for f in range(fields):
                at = pl.ds((k * fields + f) * rows + h * SUB, SUB)
                prev[f] = inc_ref[at, :] - ratio[k] * prev[f]
                inc_ref[at, :] = prev[f]


def pick(table, row, col):
    level = [jnp.take_along_axis(t, col, axis=1) for t in table]
    bit = 1
    while len(level) > 1:
        odd = (row & bit) != 0
        level = [jnp.where(odd, level[i + 1], level[i]) for i in range(0, len(level), 2)]
        bit *= 2
    return level[0]


def column_kernel(
    rows,
    layers,
    owners,
    main_ref,
    north_ref,
    south_ref,
    west_ref,
    east_ref,
    vert_ref,
    off_ref,
    w_ref,
    inc_ref,
    out_ref,
    near,
    far,
    coefs,
    off_t,
    w_t,
    acc,
):
    diffuse(rows, layers, main_ref, north_ref, south_ref, west_ref, east_ref, near, far, coefs)
    solve_columns(rows, layers, near, vert_ref, inc_ref)
    cap = off_ref.shape[1]
    groups = off_ref.shape[0] // LANES
    turns = -(-cap // layers)
    padded = turns * layers
    if padded > cap:
        for g in range(groups):
            off_t[g, cap:padded, :] = jnp.zeros((padded - cap, LANES), jnp.int32)
            w_t[g, cap:padded, :] = jnp.zeros((padded - cap, LANES), jnp.float32)
    for g in range(groups):
        for c in range(cap // LANES):
            here = pl.ds(c * LANES, LANES)
            off_t[g, here, :] = off_ref[pl.ds(g * LANES, LANES), here].T
            w_t[g, here, :] = w_ref[pl.ds(g * LANES, LANES), here].T

    def one_group(lg, carry):
        base = pl.multiple_of(lg * SUB, SUB)
        table = [inc_ref[pl.ds(base * rows + r, SUB, stride=rows), :] for r in range(rows)]
        for m in range(turns):
            at = pl.ds(m * layers + base, SUB)
            total = None
            for g in range(groups):
                idx = off_t[g, at, :]
                term = pick(table, idx >> 7, idx & (LANES - 1)) * w_t[g, at, :]
                total = term if total is None else total + term
            acc[at, :] = total
        return carry

    lax.fori_loop(0, layers // SUB, one_group, 0)
    for c in range(cap // LANES):
        here = pl.ds(c * LANES, LANES)
        block = acc[here, :].T
        total = block[:owners]
        for k in range(1, LANES // owners):
            total = total + block[k * owners : (k + 1) * owners]
        out_ref[:, here] = total


def shift(block, axis, step, closed):
    count = lax.axis_size(axis)
    pairs = [(i, (i + step) % count) for i in range(count)]
    if not closed:
        pairs = [(i, j) for i, j in pairs if j == i + step]
    return lax.ppermute(block, axis, pairs)


def local_call(kernel, shapes, count, scratch=(), name=None):
    return pl.pallas_call(
        kernel,
        out_shape=shapes,
        in_specs=[pl.BlockSpec(memory_space=pltpu.VMEM)] * count,
        out_specs=jax.tree.map(lambda _: pl.BlockSpec(memory_space=pltpu.VMEM), shapes),
        scratch_shapes=list(scratch),
        compiler_params=pltpu.CompilerParams(vmem_limit_bytes=40 * 1024 * 1024),
        name=name,
    )


def floats(*shape):
    return jax.ShapeDtypeStruct(shape, jnp.float32)


def columns_and_partials(control, kappa, sea_mask, vert_coef, offsets, weights):
    levels, fields, rows, cols = control.shape
    layers = levels * fields
    groups = layers // SUB + 1
    wide = groups * SUB
    tall = rows + 2 * STEPS
    sten, owners, cap = offsets.shape
    bundles = sten * owners // LANES
    padded = -(-cap // layers) * layers

    main = local_call(
        functools.partial(lay_kernel, rows, layers), floats(rows * wide, LANES), 3, name="lay"
    )(control.reshape(layers * rows, cols), kappa, sea_mask)
    north = shift(main[(rows - STEPS) * wide :], "lat", 1, False)
    south = shift(main[: STEPS * wide], "lat", -1, False)
    head, tail = local_call(
        functools.partial(pack_kernel, rows, groups),
        (floats(tall * SUB, LANES), floats(tall * SUB, LANES)),
        3,
        name="pack",
    )(main, north, south)
    west = shift(tail, "lon", 1, True)
    east = shift(head, "lon", -1, True)
    increment, partial_value = local_call(
        functools.partial(column_kernel, rows, layers, owners),
        (floats(layers * rows, LANES), floats(owners, cap)),
        8,
        [
            pltpu.VMEM((2, tall * layers, LANES), jnp.float32),
            pltpu.VMEM((2, tall * layers, LANES), jnp.float32),
            pltpu.VMEM((12, tall * SUB, LANES), jnp.float32),
            pltpu.VMEM((bundles, padded, LANES), jnp.int32),
            pltpu.VMEM((bundles, padded, LANES), jnp.float32),
            pltpu.VMEM((padded, LANES), jnp.float32),
        ],
        name="columns",
    )(
        main,
        north,
        south,
        west,
        east,
        vert_coef.reshape(levels * rows, cols),
        offsets.reshape(sten * owners, cap),
        weights.reshape(sten * owners, cap),
    )
    return increment.reshape(control.shape), partial_value


def split_parts(v):
    first = v.astype(jnp.bfloat16).astype(jnp.float32)
    rest = v - first
    second = rest.astype(jnp.bfloat16).astype(jnp.float32)
    return first, second, rest - second


def spread(v, t, high):
    cap = v.shape[1]
    hit = lax.broadcasted_iota(jnp.int32, (high, cap), 0) == (t >> 7)
    ones = lax.broadcasted_iota(jnp.int32, (LANES, cap), 0) == (t & (LANES - 1))
    left = jnp.concatenate(
        [jnp.where(hit, part, 0.0).astype(jnp.bfloat16) for part in split_parts(v)], axis=0
    )
    right = jnp.where(ones, 1.0, 0.0).astype(jnp.bfloat16)
    return lax.dot_general(
        left, right, (((1,), (1,)), ((), ())), preferred_element_type=jnp.float32
    )


def scatter_kernel(rec_ref, tgt_ref, obs_ref, err_ref, out_ref, acc):
    high = obs_ref.shape[0]
    acc[...] = jnp.zeros_like(acc)

    def one_source(p, carry):
        acc[...] += spread(rec_ref[pl.ds(p, 1), :], tgt_ref[pl.ds(p, 1), :], high)
        return carry

    lax.fori_loop(0, rec_ref.shape[0], one_source, 0)
    total = acc[:high] + acc[high : 2 * high] + acc[2 * high :]
    out_ref[...] = (total - obs_ref[...]) * err_ref[...]


def scatter_misfit(received, target, observed, inv_error):
    high = observed.shape[0] // LANES
    out = pl.pallas_call(
        scatter_kernel,
        out_shape=jax.ShapeDtypeStruct((high, LANES), jnp.float32),
        in_specs=[pl.BlockSpec(memory_space=pltpu.VMEM)] * 4,
        out_specs=pl.BlockSpec(memory_space=pltpu.VMEM),
        scratch_shapes=[pltpu.VMEM((3 * high, LANES), jnp.float32)],
        compiler_params=pltpu.CompilerParams(vmem_limit_bytes=32 * 1024 * 1024),
        name="scatter_misfit",
    )(received, target, observed.reshape(high, LANES), inv_error.reshape(high, LANES))
    return out.reshape(-1)


def per_device(
    control,
    kappa,
    sea_mask,
    vert_coef,
    stencil_offsets,
    stencil_weights,
    slot_target,
    observed,
    inv_error,
):
    increment, partial_value = columns_and_partials(
        control, kappa, sea_mask, vert_coef, stencil_offsets, stencil_weights
    )
    received = lax.all_to_all(
        partial_value, ("lat", "lon"), split_axis=0, concat_axis=0, tiled=True
    )
    misfit = scatter_misfit(received, slot_target, observed, inv_error)
    return (increment, misfit)


def solution(mesh):
    return jax.shard_map(
        per_device,
        mesh=mesh,
        in_specs=(
            P(None, None, "lat", "lon"),
            P("lat", "lon"),
            P("lat", "lon"),
            P(None, "lat", "lon"),
            P(None, ("lat", "lon"), None),
            P(None, ("lat", "lon"), None),
            P(("lat", "lon"), None),
            P(("lat", "lon")),
            P(("lat", "lon")),
        ),
        out_specs=(P(None, None, "lat", "lon"), P(("lat", "lon"))),
        check_vma=False,
    )
```

```python
import functools

import jax
import jax.numpy as jnp
from jax import lax
from jax.experimental import pallas as pl
from jax.experimental.pallas import tpu as pltpu
from jax.sharding import PartitionSpec as P

STEPS = 10
LANES = 128
SUB = 8


def lane_ids():
    return lax.broadcasted_iota(jnp.int32, (SUB, LANES), 1)


def lay_kernel(rows, layers, field_ref, kappa_ref, mask_ref, out_ref):
    wide = layers + SUB
    coef = kappa_ref[...] * mask_ref[...].astype(jnp.float32)
    for r in range(rows):
        for g in range(layers // SUB):
            out_ref[pl.ds(r * wide + g * SUB, SUB), :] = field_ref[
                pl.ds(g * SUB * rows + r, SUB, stride=rows), :
            ]
        out_ref[pl.ds(r * wide + layers, SUB), :] = jnp.broadcast_to(
            coef[r : r + 1, :], (SUB, LANES)
        )


def pack_kernel(rows, groups, main_ref, north_ref, south_ref, head_ref, tail_ref):
    lane = lane_ids()
    pitch = LANES // groups
    wide = groups * SUB

    def pack(src, count, start):
        def one_row(r, carry):
            base = pl.multiple_of(r * wide, SUB)
            head = jnp.zeros((SUB, LANES), jnp.float32)
            tail = head
            for g in range(groups):
                cells = src[pl.ds(base + g * SUB, SUB), :]
                spot = (lane >= g * pitch) & (lane < g * pitch + STEPS)
                head = jnp.where(spot, pltpu.roll(cells, g * pitch, 1), head)
                move = (g * pitch + STEPS) % LANES
                tail = jnp.where(spot, pltpu.roll(cells, move, 1), tail)
            at = pl.ds(pl.multiple_of((start + r) * SUB, SUB), SUB)
            head_ref[at, :] = head
            tail_ref[at, :] = tail
            return carry

        lax.fori_loop(0, count, one_row, 0, unroll=2)

    pack(north_ref, STEPS, 0)
    pack(main_ref, rows, STEPS)
    pack(south_ref, STEPS, STEPS + rows)


def diffuse(rows, layers, main_ref, north_ref, south_ref, west_ref, east_ref, near, far, near_b, far_b, coefs):
    lane = lane_ids()
    groups = layers // SUB + 1
    pitch = LANES // groups
    wide = groups * SUB
    tall = rows + 2 * STEPS

    def outer(r, g):
        at = pl.ds(pl.multiple_of(r * SUB, SUB), SUB)
        east = pltpu.roll(east_ref[at, :], (LANES - g * pitch) % LANES, 1)
        west = pltpu.roll(west_ref[at, :], (2 * LANES - STEPS - g * pitch) % LANES, 1)
        return jnp.where(lane < STEPS, east, jnp.where(lane >= LANES - STEPS, west, 0.0))

    def fill(src, count, start):
        def one_row(r, carry):
            base = pl.multiple_of(r * wide, SUB)
            row = start + r
            for g in range(groups - 1):
                at = pl.ds(pl.multiple_of(row * layers + g * SUB, SUB), SUB)
                near[at, :] = src[pl.ds(base + g * SUB, SUB), :]
                far[at, :] = outer(row, g)
            at = pl.ds(pl.multiple_of(row * SUB, SUB), SUB)
            coefs[10, at, :] = src[pl.ds(base + layers, SUB), :]
            coefs[11, at, :] = outer(row, groups - 1)
            return carry

        lax.fori_loop(0, count, one_row, 0, unroll=2)

    fill(north_ref, STEPS, 0)
    fill(main_ref, rows, STEPS)
    fill(south_ref, STEPS, STEPS + rows)

    def sides(a, b):
        ra, rb = pltpu.roll(a, 1, 1), pltpu.roll(b, 1, 1)
        la, lb = pltpu.roll(a, LANES - 1, 1), pltpu.roll(b, LANES - 1, 1)
        first, last = lane == 0, lane == LANES - 1
        return (
            (jnp.where(first, rb, ra), jnp.where(last, lb, la)),
            (jnp.where(first, ra, rb), jnp.where(last, la, lb)),
        )

    def weigh(r, carry):
        at = pl.ds(pl.multiple_of(r * SUB, SUB), SUB)
        up = pl.ds(pl.multiple_of((r - 1) * SUB, SUB), SUB)
        down = pl.ds(pl.multiple_of((r + 1) * SUB, SUB), SUB)
        both = sides(coefs[10, at, :], coefs[11, at, :])
        for k in range(2):
            here = coefs[10 + k, at, :]
            n = here * coefs[10 + k, up, :]
            s = here * coefs[10 + k, down, :]
            w = here * both[k][0]
            e = here * both[k][1]
            coefs[5 * k, at, :] = 1.0 - ((n + s) + (w + e))
            coefs[5 * k + 1, at, :] = n
            coefs[5 * k + 2, at, :] = s
            coefs[5 * k + 3, at, :] = w
            coefs[5 * k + 4, at, :] = e
        return carry

    lax.fori_loop(1, tall - 1, weigh, 0, unroll=2)

    for step in range(STEPS):
        old, new = (near, far), (near_b, far_b)
        if step % 2:
            old, new = new, old

        def one_row(r, carry, old=old, new=new):
            at = pl.ds(pl.multiple_of(r * SUB, SUB), SUB)
            c = [coefs[k, at, :] for k in range(10)]
            for g in range(groups - 1):
                mid = pl.ds(pl.multiple_of(r * layers + g * SUB, SUB), SUB)
                up = pl.ds(pl.multiple_of((r - 1) * layers + g * SUB, SUB), SUB)
                down = pl.ds(pl.multiple_of((r + 1) * layers + g * SUB, SUB), SUB)
                a, b = old[0][mid, :], old[1][mid, :]
                both = sides(a, b)
                for k, cells in enumerate((a, b)):
                    p = c[5 * k : 5 * k + 5]
                    total = p[0] * cells + p[1] * old[k][up, :]
                    other = p[3] * both[k][0] + p[4] * both[k][1]
                    new[k][mid, :] = (total + p[2] * old[k][down, :]) + other
            return carry

        lax.fori_loop(step + 1, tall - 1 - step, one_row, 0, unroll=2)


def solve_columns(rows, layers, done, vert_ref, inc_ref):
    levels = vert_ref.shape[0] // rows
    fields = layers // levels
    for h in range(rows // SUB):
        ratio = []
        coef = vert_ref[pl.ds(h * SUB, SUB), :]
        cprev = jnp.zeros((SUB, LANES), jnp.float32)
        prev = [cprev] * fields
        for k in range(levels):
            if k + 1 < levels:
                below = vert_ref[pl.ds((k + 1) * rows + h * SUB, SUB), :]
            else:
                below = jnp.zeros((SUB, LANES), jnp.float32)
            inv = 1.0 / (((1.0 + coef) + below) + coef * cprev)
            cprev = -below * inv
            ratio.append(cprev)
            for f in range(fields):
                layer = k * fields + f
                right = done[pl.ds((STEPS + h * SUB) * layers + layer, SUB, stride=layers), :]
                prev[f] = (right + coef * prev[f]) * inv
                inc_ref[pl.ds(layer * rows + h * SUB, SUB), :] = prev[f]
            coef = below
        for k in range(levels - 2, -1, -1):
            for f in range(fields):
                at = pl.ds((k * fields + f) * rows + h * SUB, SUB)
                prev[f] = inc_ref[at, :] - ratio[k] * prev[f]
                inc_ref[at, :] = prev[f]


def pick(table, row, col):
    level = [jnp.take_along_axis(t, col, axis=1) for t in table]
    bit = 1
    while len(level) > 1:
        odd = (row & bit) != 0
        level = [jnp.where(odd, level[i + 1], level[i]) for i in range(0, len(level), 2)]
        bit *= 2
    return level[0]


def turn_kernel(off_ref, w_ref, off_t, w_t):
    cap = off_ref.shape[1]
    groups = off_ref.shape[0] // LANES
    padded = off_t.shape[1]
    if padded > cap:
        for g in range(groups):
            off_t[g, cap:padded, :] = jnp.zeros((padded - cap, LANES), jnp.int32)
            w_t[g, cap:padded, :] = jnp.zeros((padded - cap, LANES), jnp.float32)
    for g in range(groups):
        for c in range(cap // LANES):
            here = pl.ds(c * LANES, LANES)
            off_t[g, here, :] = off_ref[pl.ds(g * LANES, LANES), here].T
            w_t[g, here, :] = w_ref[pl.ds(g * LANES, LANES), here].T


def column_kernel(
    rows,
    layers,
    owners,
    main_ref,
    north_ref,
    south_ref,
    west_ref,
    east_ref,
    vert_ref,
    off_t,
    w_t,
    inc_ref,
    out_ref,
    near,
    far,
    near_b,
    far_b,
    coefs,
    acc,
):
    diffuse(
        rows, layers, main_ref, north_ref, south_ref, west_ref, east_ref, near, far, near_b, far_b, coefs
    )
    solve_columns(rows, layers, near_b if STEPS % 2 else near, vert_ref, inc_ref)
    cap = out_ref.shape[1]
    groups = off_t.shape[0]
    turns = -(-cap // layers)

    def one_group(lg, carry):
        base = pl.multiple_of(lg * SUB, SUB)
        table = [inc_ref[pl.ds(base * rows + r, SUB, stride=rows), :] for r in range(rows)]
        for m in range(turns):
            at = pl.ds(m * layers + base, SUB)
            total = None
            for g in range(groups):
                idx = off_t[g, at, :]
                term = pick(table, idx >> 7, idx & (LANES - 1)) * w_t[g, at, :]
                total = term if total is None else total + term
            acc[at, :] = total
        return carry

    lax.fori_loop(0, layers // SUB, one_group, 0, unroll=2)
    for c in range(cap // LANES):
        here = pl.ds(c * LANES, LANES)
        block = acc[here, :].T
        total = block[:owners]
        for k in range(1, LANES // owners):
            total = total + block[k * owners : (k + 1) * owners]
        out_ref[:, here] = total


def shift(block, axis, step, closed):
    count = lax.axis_size(axis)
    pairs = [(i, (i + step) % count) for i in range(count)]
    if not closed:
        pairs = [(i, j) for i, j in pairs if j == i + step]
    return lax.ppermute(block, axis, pairs)


def local_call(kernel, shapes, count, scratch=(), name=None):
    return pl.pallas_call(
        kernel,
        out_shape=shapes,
        in_specs=[pl.BlockSpec(memory_space=pltpu.VMEM)] * count,
        out_specs=jax.tree.map(lambda _: pl.BlockSpec(memory_space=pltpu.VMEM), shapes),
        scratch_shapes=list(scratch),
        compiler_params=pltpu.CompilerParams(vmem_limit_bytes=40 * 1024 * 1024),
        name=name,
    )


def floats(*shape):
    return jax.ShapeDtypeStruct(shape, jnp.float32)


def columns_and_partials(control, kappa, sea_mask, vert_coef, offsets, weights):
    levels, fields, rows, cols = control.shape
    layers = levels * fields
    groups = layers // SUB + 1
    wide = groups * SUB
    tall = rows + 2 * STEPS
    sten, owners, cap = offsets.shape
    bundles = sten * owners // LANES
    padded = -(-cap // layers) * layers

    main = local_call(
        functools.partial(lay_kernel, rows, layers), floats(rows * wide, LANES), 3, name="lay"
    )(control.reshape(layers * rows, cols), kappa, sea_mask)
    north = shift(main[(rows - STEPS) * wide :], "lat", 1, False)
    south = shift(main[: STEPS * wide], "lat", -1, False)
    head, tail = local_call(
        functools.partial(pack_kernel, rows, groups),
        (floats(tall * SUB, LANES), floats(tall * SUB, LANES)),
        3,
        name="pack",
    )(main, north, south)
    west = shift(tail, "lon", 1, True)
    east = shift(head, "lon", -1, True)
    off_t, w_t = local_call(
        turn_kernel,
        (
            jax.ShapeDtypeStruct((bundles, padded, LANES), jnp.int32),
            floats(bundles, padded, LANES),
        ),
        2,
        name="turn",
    )(offsets.reshape(sten * owners, cap), weights.reshape(sten * owners, cap))
    increment, partial_value = local_call(
        functools.partial(column_kernel, rows, layers, owners),
        (floats(layers * rows, LANES), floats(owners, cap)),
        8,
        [
            pltpu.VMEM((tall * layers, LANES), jnp.float32),
            pltpu.VMEM((tall * layers, LANES), jnp.float32),
            pltpu.VMEM((tall * layers, LANES), jnp.float32),
            pltpu.VMEM((tall * layers, LANES), jnp.float32),
            pltpu.VMEM((12, tall * SUB, LANES), jnp.float32),
            pltpu.VMEM((padded, LANES), jnp.float32),
        ],
        name="columns",
    )(
        main,
        north,
        south,
        west,
        east,
        vert_coef.reshape(levels * rows, cols),
        off_t,
        w_t,
    )
    return increment.reshape(control.shape), partial_value


def split_parts(v):
    first = v.astype(jnp.bfloat16).astype(jnp.float32)
    rest = v - first
    second = rest.astype(jnp.bfloat16).astype(jnp.float32)
    return first, second, rest - second


def spread(v, t, high):
    cap = v.shape[1]
    hit = lax.broadcasted_iota(jnp.int32, (high, cap), 0) == (t >> 7)
    ones = lax.broadcasted_iota(jnp.int32, (LANES, cap), 0) == (t & (LANES - 1))
    left = jnp.concatenate(
        [jnp.where(hit, part, 0.0).astype(jnp.bfloat16) for part in split_parts(v)], axis=0
    )
    right = jnp.where(ones, 1.0, 0.0).astype(jnp.bfloat16)
    return lax.dot_general(
        left, right, (((1,), (1,)), ((), ())), preferred_element_type=jnp.float32
    )


def scatter_kernel(rec_ref, tgt_ref, obs_ref, err_ref, out_ref, acc):
    high = obs_ref.shape[0]
    acc[...] = jnp.zeros_like(acc)

    def one_source(p, carry):
        acc[...] += spread(rec_ref[pl.ds(p, 1), :], tgt_ref[pl.ds(p, 1), :], high)
        return carry

    lax.fori_loop(0, rec_ref.shape[0], one_source, 0, unroll=4)
    total = acc[:high] + acc[high : 2 * high] + acc[2 * high :]
    out_ref[...] = (total - obs_ref[...]) * err_ref[...]


def scatter_misfit(received, target, observed, inv_error):
    high = observed.shape[0] // LANES
    out = pl.pallas_call(
        scatter_kernel,
        out_shape=jax.ShapeDtypeStruct((high, LANES), jnp.float32),
        in_specs=[pl.BlockSpec(memory_space=pltpu.VMEM)] * 4,
        out_specs=pl.BlockSpec(memory_space=pltpu.VMEM),
        scratch_shapes=[pltpu.VMEM((3 * high, LANES), jnp.float32)],
        compiler_params=pltpu.CompilerParams(vmem_limit_bytes=32 * 1024 * 1024),
        name="scatter_misfit",
    )(received, target, observed.reshape(high, LANES), inv_error.reshape(high, LANES))
    return out.reshape(-1)


def per_device(
    control,
    kappa,
    sea_mask,
    vert_coef,
    stencil_offsets,
    stencil_weights,
    slot_target,
    observed,
    inv_error,
):
    increment, partial_value = columns_and_partials(
        control, kappa, sea_mask, vert_coef, stencil_offsets, stencil_weights
    )
    received = lax.all_to_all(
        partial_value, ("lat", "lon"), split_axis=0, concat_axis=0, tiled=True
    )
    misfit = scatter_misfit(received, slot_target, observed, inv_error)
    return (increment, misfit)


def solution(mesh):
    return jax.shard_map(
        per_device,
        mesh=mesh,
        in_specs=(
            P(None, None, "lat", "lon"),
            P("lat", "lon"),
            P("lat", "lon"),
            P(None, "lat", "lon"),
            P(None, ("lat", "lon"), None),
            P(None, ("lat", "lon"), None),
            P(("lat", "lon"), None),
            P(("lat", "lon")),
            P(("lat", "lon")),
        ),
        out_specs=(P(None, None, "lat", "lon"), P(("lat", "lon"))),
        check_vma=False,
    )
```

```python
import functools

import jax
import jax.numpy as jnp
from jax import lax
from jax.experimental import pallas as pl
from jax.experimental.pallas import tpu as pltpu
from jax.sharding import PartitionSpec as P

STEPS = 10
LANES = 128
SUB = 8


def lane_ids():
    return lax.broadcasted_iota(jnp.int32, (SUB, LANES), 1)


def lay_kernel(rows, layers, field_ref, kappa_ref, mask_ref, out_ref):
    wide = layers + SUB
    coef = kappa_ref[...] * mask_ref[...].astype(jnp.float32)
    for r in range(rows):
        for g in range(layers // SUB):
            out_ref[pl.ds(r * wide + g * SUB, SUB), :] = field_ref[
                pl.ds(g * SUB * rows + r, SUB, stride=rows), :
            ]
        out_ref[pl.ds(r * wide + layers, SUB), :] = jnp.broadcast_to(
            coef[r : r + 1, :], (SUB, LANES)
        )


def pack_kernel(rows, groups, main_ref, north_ref, south_ref, head_ref, tail_ref):
    lane = lane_ids()
    pitch = LANES // groups
    wide = groups * SUB

    def pack(src, count, start):
        def one_row(r, carry):
            base = pl.multiple_of(r * wide, SUB)
            head = jnp.zeros((SUB, LANES), jnp.float32)
            tail = head
            for g in range(groups):
                cells = src[pl.ds(base + g * SUB, SUB), :]
                spot = (lane >= g * pitch) & (lane < g * pitch + STEPS)
                head = jnp.where(spot, pltpu.roll(cells, g * pitch, 1), head)
                move = (g * pitch + STEPS) % LANES
                tail = jnp.where(spot, pltpu.roll(cells, move, 1), tail)
            at = pl.ds(pl.multiple_of((start + r) * SUB, SUB), SUB)
            head_ref[at, :] = head
            tail_ref[at, :] = tail
            return carry

        lax.fori_loop(0, count, one_row, 0, unroll=2)

    pack(north_ref, STEPS, 0)
    pack(main_ref, rows, STEPS)
    pack(south_ref, STEPS, STEPS + rows)


def diffuse(rows, layers, main_ref, north_ref, south_ref, west_ref, east_ref, near, far, near_b, far_b, coefs):
    lane = lane_ids()
    groups = layers // SUB + 1
    pitch = LANES // groups
    wide = groups * SUB
    tall = rows + 2 * STEPS

    def outer(r, g):
        at = pl.ds(pl.multiple_of(r * SUB, SUB), SUB)
        east = pltpu.roll(east_ref[at, :], (LANES - g * pitch) % LANES, 1)
        west = pltpu.roll(west_ref[at, :], (2 * LANES - STEPS - g * pitch) % LANES, 1)
        return jnp.where(lane < STEPS, east, jnp.where(lane >= LANES - STEPS, west, 0.0))

    def fill(src, count, start):
        def one_row(r, carry):
            base = pl.multiple_of(r * wide, SUB)
            row = start + r
            for g in range(groups - 1):
                at = pl.ds(pl.multiple_of(row * layers + g * SUB, SUB), SUB)
                near[at, :] = src[pl.ds(base + g * SUB, SUB), :]
                far[at, :] = outer(row, g)
            at = pl.ds(pl.multiple_of(row * SUB, SUB), SUB)
            coefs[10, at, :] = src[pl.ds(base + layers, SUB), :]
            coefs[11, at, :] = outer(row, groups - 1)
            return carry

        lax.fori_loop(0, count, one_row, 0, unroll=2)

    fill(north_ref, STEPS, 0)
    fill(main_ref, rows, STEPS)
    fill(south_ref, STEPS, STEPS + rows)

    def sides(a, b):
        ra, rb = pltpu.roll(a, 1, 1), pltpu.roll(b, 1, 1)
        la, lb = pltpu.roll(a, LANES - 1, 1), pltpu.roll(b, LANES - 1, 1)
        first, last = lane == 0, lane == LANES - 1
        return (
            (jnp.where(first, rb, ra), jnp.where(last, lb, la)),
            (jnp.where(first, ra, rb), jnp.where(last, la, lb)),
        )

    def weigh(r, carry):
        at = pl.ds(pl.multiple_of(r * SUB, SUB), SUB)
        up = pl.ds(pl.multiple_of((r - 1) * SUB, SUB), SUB)
        down = pl.ds(pl.multiple_of((r + 1) * SUB, SUB), SUB)
        both = sides(coefs[10, at, :], coefs[11, at, :])
        for k in range(2):
            here = coefs[10 + k, at, :]
            n = here * coefs[10 + k, up, :]
            s = here * coefs[10 + k, down, :]
            w = here * both[k][0]
            e = here * both[k][1]
            coefs[5 * k, at, :] = 1.0 - ((n + s) + (w + e))
            coefs[5 * k + 1, at, :] = n
            coefs[5 * k + 2, at, :] = s
            coefs[5 * k + 3, at, :] = w
            coefs[5 * k + 4, at, :] = e
        return carry

    lax.fori_loop(1, tall - 1, weigh, 0, unroll=2)

    for step in range(STEPS):
        old, new = (near, far), (near_b, far_b)
        if step % 2:
            old, new = new, old

        def two_rows(turn, carry, old=old, new=new, first=step + 1):
            r = first + 2 * turn
            c = [
                [coefs[k, pl.ds(pl.multiple_of((r + d) * SUB, SUB), SUB), :] for k in range(10)]
                for d in range(2)
            ]
            for g in range(groups - 1):
                spots = [
                    pl.ds(pl.multiple_of((r + d) * layers + g * SUB, SUB), SUB)
                    for d in range(-1, 3)
                ]
                cells = [[old[k][spot, :] for spot in spots] for k in range(2)]
                results = []
                for d in range(2):
                    both = sides(cells[0][d + 1], cells[1][d + 1])
                    for k in range(2):
                        p = c[d][5 * k : 5 * k + 5]
                        total = p[0] * cells[k][d + 1] + p[1] * cells[k][d]
                        other = p[3] * both[k][0] + p[4] * both[k][1]
                        results.append((k, spots[d + 1], (total + p[2] * cells[k][d + 2]) + other))
                for k, spot, value in results:
                    new[k][spot, :] = value
            return carry

        lax.fori_loop(0, (tall - 2 - 2 * step) // 2, two_rows, 0)


def solve_columns(rows, layers, done, vert_ref, inc_ref):
    levels = vert_ref.shape[0] // rows
    fields = layers // levels
    for h in range(rows // SUB):
        ratio = []
        coef = vert_ref[pl.ds(h * SUB, SUB), :]
        cprev = jnp.zeros((SUB, LANES), jnp.float32)
        prev = [cprev] * fields
        for k in range(levels):
            if k + 1 < levels:
                below = vert_ref[pl.ds((k + 1) * rows + h * SUB, SUB), :]
            else:
                below = jnp.zeros((SUB, LANES), jnp.float32)
            inv = 1.0 / (((1.0 + coef) + below) + coef * cprev)
            cprev = -below * inv
            ratio.append(cprev)
            for f in range(fields):
                layer = k * fields + f
                right = done[pl.ds((STEPS + h * SUB) * layers + layer, SUB, stride=layers), :]
                prev[f] = (right + coef * prev[f]) * inv
                inc_ref[pl.ds(layer * rows + h * SUB, SUB), :] = prev[f]
            coef = below
        for k in range(levels - 2, -1, -1):
            for f in range(fields):
                at = pl.ds((k * fields + f) * rows + h * SUB, SUB)
                prev[f] = inc_ref[at, :] - ratio[k] * prev[f]
                inc_ref[at, :] = prev[f]


def pick(table, row, col):
    level = [jnp.take_along_axis(t, col, axis=1) for t in table]
    bit = 1
    while len(level) > 1:
        odd = (row & bit) != 0
        level = [jnp.where(odd, level[i + 1], level[i]) for i in range(0, len(level), 2)]
        bit *= 2
    return level[0]


def turn_kernel(off_ref, w_ref, off_t, w_t):
    cap = off_ref.shape[1]
    groups = off_ref.shape[0] // LANES
    padded = off_t.shape[1]
    if padded > cap:
        for g in range(groups):
            off_t[g, cap:padded, :] = jnp.zeros((padded - cap, LANES), jnp.int32)
            w_t[g, cap:padded, :] = jnp.zeros((padded - cap, LANES), jnp.float32)
    for g in range(groups):
        for c in range(cap // LANES):
            here = pl.ds(c * LANES, LANES)
            off_t[g, here, :] = off_ref[pl.ds(g * LANES, LANES), here].T
            w_t[g, here, :] = w_ref[pl.ds(g * LANES, LANES), here].T


def column_kernel(
    rows,
    layers,
    owners,
    main_ref,
    north_ref,
    south_ref,
    west_ref,
    east_ref,
    vert_ref,
    off_t,
    w_t,
    inc_ref,
    out_ref,
    near,
    far,
    near_b,
    far_b,
    coefs,
    acc,
):
    diffuse(
        rows, layers, main_ref, north_ref, south_ref, west_ref, east_ref, near, far, near_b, far_b, coefs
    )
    solve_columns(rows, layers, near_b if STEPS % 2 else near, vert_ref, inc_ref)
    cap = out_ref.shape[1]
    groups = off_t.shape[0]
    turns = -(-cap // layers)

    def one_group(lg, carry):
        base = pl.multiple_of(lg * SUB, SUB)
        table = [inc_ref[pl.ds(base * rows + r, SUB, stride=rows), :] for r in range(rows)]
        for m in range(turns):
            at = pl.ds(m * layers + base, SUB)
            total = None
            for g in range(groups):
                idx = off_t[g, at, :]
                term = pick(table, idx >> 7, idx & (LANES - 1)) * w_t[g, at, :]
                total = term if total is None else total + term
            acc[at, :] = total
        return carry

    lax.fori_loop(0, layers // SUB, one_group, 0, unroll=2)
    for c in range(cap // LANES):
        here = pl.ds(c * LANES, LANES)
        block = acc[here, :].T
        total = block[:owners]
        for k in range(1, LANES // owners):
            total = total + block[k * owners : (k + 1) * owners]
        out_ref[:, here] = total


def shift(block, axis, step, closed):
    count = lax.axis_size(axis)
    pairs = [(i, (i + step) % count) for i in range(count)]
    if not closed:
        pairs = [(i, j) for i, j in pairs if j == i + step]
    return lax.ppermute(block, axis, pairs)


def local_call(kernel, shapes, count, scratch=(), name=None):
    return pl.pallas_call(
        kernel,
        out_shape=shapes,
        in_specs=[pl.BlockSpec(memory_space=pltpu.VMEM)] * count,
        out_specs=jax.tree.map(lambda _: pl.BlockSpec(memory_space=pltpu.VMEM), shapes),
        scratch_shapes=list(scratch),
        compiler_params=pltpu.CompilerParams(vmem_limit_bytes=40 * 1024 * 1024),
        name=name,
    )


def floats(*shape):
    return jax.ShapeDtypeStruct(shape, jnp.float32)


def columns_and_partials(control, kappa, sea_mask, vert_coef, offsets, weights):
    levels, fields, rows, cols = control.shape
    layers = levels * fields
    groups = layers // SUB + 1
    wide = groups * SUB
    tall = rows + 2 * STEPS
    sten, owners, cap = offsets.shape
    bundles = sten * owners // LANES
    padded = -(-cap // layers) * layers

    main = local_call(
        functools.partial(lay_kernel, rows, layers), floats(rows * wide, LANES), 3, name="lay"
    )(control.reshape(layers * rows, cols), kappa, sea_mask)
    north = shift(main[(rows - STEPS) * wide :], "lat", 1, False)
    south = shift(main[: STEPS * wide], "lat", -1, False)
    head, tail = local_call(
        functools.partial(pack_kernel, rows, groups),
        (floats(tall * SUB, LANES), floats(tall * SUB, LANES)),
        3,
        name="pack",
    )(main, north, south)
    west = shift(tail, "lon", 1, True)
    east = shift(head, "lon", -1, True)
    off_t, w_t = local_call(
        turn_kernel,
        (
            jax.ShapeDtypeStruct((bundles, padded, LANES), jnp.int32),
            floats(bundles, padded, LANES),
        ),
        2,
        name="turn",
    )(offsets.reshape(sten * owners, cap), weights.reshape(sten * owners, cap))
    increment, partial_value = local_call(
        functools.partial(column_kernel, rows, layers, owners),
        (floats(layers * rows, LANES), floats(owners, cap)),
        8,
        [
            pltpu.VMEM((tall * layers, LANES), jnp.float32),
            pltpu.VMEM((tall * layers, LANES), jnp.float32),
            pltpu.VMEM((tall * layers, LANES), jnp.float32),
            pltpu.VMEM((tall * layers, LANES), jnp.float32),
            pltpu.VMEM((12, tall * SUB, LANES), jnp.float32),
            pltpu.VMEM((padded, LANES), jnp.float32),
        ],
        name="columns",
    )(
        main,
        north,
        south,
        west,
        east,
        vert_coef.reshape(levels * rows, cols),
        off_t,
        w_t,
    )
    return increment.reshape(control.shape), partial_value


def split_parts(v):
    first = v.astype(jnp.bfloat16).astype(jnp.float32)
    rest = v - first
    second = rest.astype(jnp.bfloat16).astype(jnp.float32)
    return first, second, rest - second


def spread(v, t, high):
    cap = v.shape[1]
    hit = lax.broadcasted_iota(jnp.int32, (high, cap), 0) == (t >> 7)
    ones = lax.broadcasted_iota(jnp.int32, (LANES, cap), 0) == (t & (LANES - 1))
    left = jnp.concatenate(
        [jnp.where(hit, part, 0.0).astype(jnp.bfloat16) for part in split_parts(v)], axis=0
    )
    right = jnp.where(ones, 1.0, 0.0).astype(jnp.bfloat16)
    return lax.dot_general(
        left, right, (((1,), (1,)), ((), ())), preferred_element_type=jnp.float32
    )


def scatter_kernel(rec_ref, tgt_ref, obs_ref, err_ref, out_ref, acc):
    high = obs_ref.shape[0]
    acc[...] = jnp.zeros_like(acc)

    def one_source(p, carry):
        acc[...] += spread(rec_ref[pl.ds(p, 1), :], tgt_ref[pl.ds(p, 1), :], high)
        return carry

    lax.fori_loop(0, rec_ref.shape[0], one_source, 0, unroll=8)
    total = acc[:high] + acc[high : 2 * high] + acc[2 * high :]
    out_ref[...] = (total - obs_ref[...]) * err_ref[...]


def scatter_misfit(received, target, observed, inv_error):
    high = observed.shape[0] // LANES
    out = pl.pallas_call(
        scatter_kernel,
        out_shape=jax.ShapeDtypeStruct((high, LANES), jnp.float32),
        in_specs=[pl.BlockSpec(memory_space=pltpu.VMEM)] * 4,
        out_specs=pl.BlockSpec(memory_space=pltpu.VMEM),
        scratch_shapes=[pltpu.VMEM((3 * high, LANES), jnp.float32)],
        compiler_params=pltpu.CompilerParams(vmem_limit_bytes=32 * 1024 * 1024),
        name="scatter_misfit",
    )(received, target, observed.reshape(high, LANES), inv_error.reshape(high, LANES))
    return out.reshape(-1)


def per_device(
    control,
    kappa,
    sea_mask,
    vert_coef,
    stencil_offsets,
    stencil_weights,
    slot_target,
    observed,
    inv_error,
):
    increment, partial_value = columns_and_partials(
        control, kappa, sea_mask, vert_coef, stencil_offsets, stencil_weights
    )
    received = lax.all_to_all(
        partial_value, ("lat", "lon"), split_axis=0, concat_axis=0, tiled=True
    )
    misfit = scatter_misfit(received, slot_target, observed, inv_error)
    return (increment, misfit)


def solution(mesh):
    return jax.shard_map(
        per_device,
        mesh=mesh,
        in_specs=(
            P(None, None, "lat", "lon"),
            P("lat", "lon"),
            P("lat", "lon"),
            P(None, "lat", "lon"),
            P(None, ("lat", "lon"), None),
            P(None, ("lat", "lon"), None),
            P(("lat", "lon"), None),
            P(("lat", "lon")),
            P(("lat", "lon")),
        ),
        out_specs=(P(None, None, "lat", "lon"), P(("lat", "lon"))),
        check_vma=False,
    )
```
